32 devices in a mesh: rep: 4 (over y, core), vol: 8 (over z, x).
Axes of the slice: x: 2, y: 2, z: 4, core: 2. Of those that a mesh axis runs over, the one named last changes fastest.
Arguments:
- positions: float32 [8192, 2, 24], P(('rep', 'vol')), may hold values from -1 to 1
- spacing: float32 [8192, 2, 8], P(('rep', 'vol')), may hold values from 0.05 to 0.5
- volume_ids: int32 [8192, 2], P(('rep', 'vol')), may hold values from 0 to 31, all different within a row; in each aligned block of 256 rows (0 to 255, 256 to 511, ...) at most 32 rows name the same one
- target: float32 [3, 8192], P(None, ('rep', 'vol')), may hold values from 0 to 1
- w_in: bfloat16 [32, 64, 256], P('vol'), may hold values from -0.75 to 0.75
- w_hidden: bfloat16 [32, 256, 256], P('vol'), may hold values from -0.375 to 0.375
- w_head: bfloat16 [32, 4, 256], P('vol'), may hold values from -0.375 to 0.375
Outputs:
- rendered: float32 [3, 8192], P(None, ('rep', 'vol'))
- grad_in: float32 [32, 64, 256], P('vol', None, 'rep')
- grad_hidden: float32 [32, 256, 256], P('vol', 'rep')
- grad_head: float32 [32, 4, 256], P('vol', None, 'rep')
The draws below stay inside these ranges and needn't reach their ends.
Inputs may be any that keep to these rules, and one draw needn't show every extreme that they name: `volume_ids`: the 2 entries of a ray are different sub-volumes, nearest first. Among the 256 rays of one device no sub-volume is named more than 32 times, and in some device's rays one is named exactly 32 times.
All inputs are finite; a program needn't handle non-finite values.
Results may differ from the reference program's by a relative error of at most 0.012.
Values may be sent and summed in bfloat16 or wider, within the bound.
No kernel may reach another device: no remote copies, remote signals or barrier semaphores. Data moves between devices by JAX's collectives and lax.ppermute only.
A program may use at most 64 MiB of HBM per device.

```python
import math
import jax
import jax.numpy as jnp
import numpy as np
from jax import lax

FREQS = 10
ENC = 64
WIDTH = 256
TOP = 2
SAMPLES = 8
RAYS_DEV = 256
VOLUMES = 32
RAYS = 8192
CAP = 32
N_REP = 4
N_VOL = 8


def levels(rng, shape, shards, smallest, top_value):
    loudness = 1.0
    for position, parts in shards:
        draws = jax.random.uniform(jax.random.fold_in(jax.random.fold_in(rng, 6), position), (parts,), jnp.float32, smallest / len(shards), top_value / len(shards))
        loudness = loudness * jnp.repeat(jnp.exp(draws), shape[position] // parts).reshape((-1,) + (1,) * (len(shape) - 1 - position))
    return loudness


def shared_out(own_key, own, number, rows, count, top, bound, skew):
    sequence = jax.random.permutation(own_key, count)
    heavy_load, ordinary = load_shares(count, rows * top, bound, skew, True), load_shares(count, rows * top, bound, skew, False)
    places = jnp.arange(count)

    def named(sizes, offset_by):
        used = int((sizes > 0).sum())
        fixed = max(1, used // 4)
        passed = fixed + (places - fixed + offset_by * (used - fixed)) % max(1, count - fixed)
        return jnp.zeros((count,), jnp.int32).at[sequence[jnp.where(places < fixed, places, passed)]].set(jnp.asarray(sizes, jnp.int32))

    sizes = jnp.where(number % 4 == 0, named(heavy_load, number // 4), named(ordinary, number - number // 4 - 1))
    mixed = jax.random.permutation(jax.random.fold_in(own, 3), count)
    giver, receiver = mixed[0:count // 2 * 2:2], mixed[1:count // 2 * 2:2]
    margin = jnp.minimum(sizes[giver] - 1, bound - sizes[receiver]) // 2
    margin = jnp.where((giver == sequence[0]) | (receiver == sequence[0]) | (sizes[receiver] == 0), 0, jnp.maximum(margin, 0))
    passed = jax.random.randint(jax.random.fold_in(own, 4), (count // 2,), 0, 1 << 20) % (margin + 1)
    sizes = sizes.at[giver].add(-passed).at[receiver].add(passed)
    labels = jnp.searchsorted(jnp.cumsum(sizes), jnp.arange(rows * top), side="right").astype(jnp.int32)
    table = labels.reshape(top, rows).T
    table = table[jax.random.permutation(jax.random.fold_in(own, 1), rows)]
    offset_by = jax.random.randint(jax.random.fold_in(own, 2), (rows, 1), 0, top)
    return jnp.take_along_axis(table, (jnp.arange(top)[None, :] + offset_by) % top, axis=1)


def load_shares(amount, total, bound, lean, full):
    portions = [(1 << 20) // math.isqrt(grade ** lean) + 1 for grade in range(1, amount + 1)]
    largest = bound if full else min(bound, max(-(-total // amount), total * portions[0] // sum(portions)))
    least = 1 if total - largest >= amount - 1 else 0
    given, surplus = [largest] + [least] * (amount - 1), total - largest - least * (amount - 1)
    while surplus > 0:
        candidates = [i for i in range(1, amount) if given[i] < largest] or [i for i in range(1, amount) if given[i] < bound]
        whole, remaining = sum([portions[i] for i in candidates]), surplus
        for i in candidates:
            extra = min(bound - given[i], max(1, remaining * portions[i] // whole), surplus)
            given[i] = given[i] + extra
            surplus = surplus - extra
    return np.array(given)


def noise(stream_key, shape, deviation, limit, cuts=(), held_as=jnp.bfloat16):
    entries = deviation * jax.random.normal(stream_key, shape, jnp.float32)
    if cuts:
        entries = entries * levels(stream_key, shape, cuts, -0.22, 0.18)
    return jnp.clip(entries, -limit, limit).astype(held_as)


def setup_inputs(seed: int = 0) -> dict:
    key_list = jax.random.split(jax.random.key(seed), 8)
    positions = jnp.clip(jax.random.uniform(key_list[0], (RAYS, TOP, 3 * SAMPLES), jnp.float32, -1.0, 1.0) * levels(key_list[0], (RAYS, TOP, 3 * SAMPLES), ((0, 32),), -0.4, 0.0), -1.0, 1.0)
    spacing = jnp.clip(jnp.exp(math.log(0.5) - 2.3025851 * jax.random.uniform(key_list[1], (RAYS, TOP, SAMPLES), jnp.float32) ** levels(key_list[1], (RAYS, TOP, SAMPLES), ((0, 32),), -0.2, 0.2)), 0.05, 0.5)
    volume_ids_keys = jax.random.split(jax.random.fold_in(key_list[2], 1), RAYS // RAYS_DEV)
    volume_ids_turns = jax.random.permutation(jax.random.fold_in(key_list[2], 3), RAYS // RAYS_DEV)
    volume_ids = jax.vmap(lambda own, number: shared_out(jax.random.fold_in(key_list[2], 2), own, number, RAYS_DEV, VOLUMES, TOP, CAP, 2))(volume_ids_keys, volume_ids_turns).reshape((RAYS, TOP))
    target = jnp.clip(1.0 * jax.random.uniform(key_list[3], (3, RAYS), jnp.float32) ** levels(key_list[3], (3, RAYS), ((1, 32),), -0.2, 0.2), 0.0, 1.0)
    w_in = noise(key_list[4], (VOLUMES, ENC, WIDTH), ENC ** -0.5, 0.75, ((0, 8),))
    w_hidden = noise(key_list[5], (VOLUMES, WIDTH, WIDTH), WIDTH ** -0.5, 0.375, ((0, 8),))
    w_head = noise(key_list[6], (VOLUMES, 4, WIDTH), WIDTH ** -0.5, 0.375, ((0, 8),))
    return {"positions": positions, "spacing": spacing, "volume_ids": volume_ids, "target": target, "w_in": w_in, "w_hidden": w_hidden, "w_head": w_head}


def encode(points):
    coords = jnp.swapaxes(points, -1, -2)
    scales = (2.0 ** jnp.arange(FREQS)).astype(coords.dtype) * math.pi
    angles = (coords[..., None] * scales).reshape(coords.shape[:-1] + (3 * FREQS,))
    unit = jnp.ones(coords.shape[:-1] + (1,), coords.dtype)
    return jnp.concatenate([jnp.sin(angles), jnp.cos(angles), coords, unit], axis=-1)

def silu_slope(pre_act):
    gate = jax.nn.sigmoid(pre_act)
    return gate * (1.0 + pre_act * (1.0 - gate))

def product(left, right):
    return jnp.dot(left.astype(jnp.float32), right.astype(jnp.float32), preferred_element_type=jnp.float32)

def forward(rows, w_first, w_mid, w_last):
    pre_one = product(rows, w_first)
    act_one = jax.nn.silu(pre_one).astype(jnp.bfloat16)
    pre_two = product(act_one, w_mid)
    act_two = jax.nn.silu(pre_two).astype(jnp.bfloat16)
    raw_out = product(act_two, w_last.T)
    return (pre_one, act_one, pre_two, act_two, raw_out)

def activate(raw_out):
    return jnp.concatenate([jax.nn.sigmoid(raw_out[:, :3]), jax.nn.softplus(raw_out[:, 3:])], axis=1)

def backward(rows, cotangent, w_first, w_mid, w_last):
    pre_one, act_one, pre_two, act_two, raw_out = forward(rows, w_first, w_mid, w_last)
    gate = jax.nn.sigmoid(raw_out)
    slope = jnp.concatenate([gate[:, :3] * (1.0 - gate[:, :3]), gate[:, 3:]], axis=1)
    cot_raw = (cotangent * slope).astype(jnp.bfloat16)
    d_last = product(cot_raw.T, act_two)
    cot_two = (product(cot_raw, w_last) * silu_slope(pre_two)).astype(jnp.bfloat16)
    d_mid = product(act_one.T, cot_two)
    cot_one = (product(cot_two, w_mid.T) * silu_slope(pre_one)).astype(jnp.bfloat16)
    d_first = product(rows.T, cot_one)
    return (d_first, d_mid, d_last)

def slots_of(volume_ids, volume_count, capacity):
    flat_ids = volume_ids.reshape(-1)
    table = (flat_ids[:, None] == jnp.arange(volume_count, dtype=jnp.int32)[None, :]).astype(jnp.int32)
    earlier = jnp.cumsum(table, axis=0) - table
    return flat_ids * capacity + lax.optimization_barrier(jnp.sum(earlier * table, axis=1))

def render(radiance, spacing):
    tau = radiance[..., 3] * spacing
    alpha = 1.0 - jnp.exp(-tau)
    before = jnp.cumsum(tau, axis=-1) - tau
    share = jnp.exp(-before) * alpha
    seg_color = lax.optimization_barrier(jnp.sum(share[..., None] * radiance[..., :3], axis=-2))
    passing = jnp.exp(-lax.optimization_barrier(jnp.sum(tau, axis=-1)))
    color = seg_color[:, 0]
    carried = passing[:, 0]
    for segment in range(1, passing.shape[1]):
        color = color + carried[:, None] * seg_color[:, segment]
        carried = carried * passing[:, segment]
    return color.T

def reference(positions, spacing, volume_ids, target, w_in, w_hidden, w_head):
    group_pos = positions.reshape(N_REP, N_VOL, RAYS_DEV * TOP, 3, SAMPLES)
    group_gap = spacing.reshape(N_REP, N_VOL, RAYS_DEV, TOP, SAMPLES)
    group_ids = volume_ids.reshape(N_REP, N_VOL, RAYS_DEV, TOP)
    group_tgt = jnp.transpose(target.reshape(3, N_REP, N_VOL, RAYS_DEV), (1, 2, 0, 3))
    row_count = N_VOL * CAP * SAMPLES

    def one_group(totals, pieces):
        points, gaps, chosen_ids, wanted = pieces
        places = jax.vmap(lambda chosen: slots_of(chosen, VOLUMES, CAP))(chosen_ids)
        feats = encode(points).astype(jnp.bfloat16).reshape(N_VOL, RAYS_DEV * TOP, SAMPLES * ENC)
        empty_feat = jnp.zeros((VOLUMES * CAP, SAMPLES * ENC), jnp.bfloat16)
        buffers = jax.vmap(lambda spots, values: empty_feat.at[spots].set(values))(places, feats)
        rows = jnp.swapaxes(buffers.reshape(N_VOL, VOLUMES, CAP * SAMPLES, ENC), 0, 1).reshape(VOLUMES, row_count, ENC)
        radiance = lax.map(lambda item: activate(forward(*item)[4]), (rows, w_in, w_hidden, w_head))
        returned = jnp.swapaxes(radiance.reshape(VOLUMES, N_VOL, CAP * SAMPLES * 4), 0, 1)
        returned = returned.reshape(N_VOL, VOLUMES * CAP, SAMPLES, 4)
        per_ray = jax.vmap(lambda stored, spots: stored[spots])(returned, places)
        per_ray = per_ray.reshape(N_VOL, RAYS_DEV, TOP, SAMPLES, 4)
        color, pull = jax.vjp(lambda values: jax.vmap(render)(values, gaps), per_ray)
        cot_ray, = pull((color - wanted) / N_REP)
        empty_cot = jnp.zeros((VOLUMES * CAP, SAMPLES * 4), cot_ray.dtype)
        cot_flat = cot_ray.reshape(N_VOL, RAYS_DEV * TOP, SAMPLES * 4)
        cot_buffers = jax.vmap(lambda spots, values: empty_cot.at[spots].set(values))(places, cot_flat)
        cot_rows = jnp.swapaxes(cot_buffers.reshape(N_VOL, VOLUMES, CAP * SAMPLES * 4), 0, 1)
        cot_rows = cot_rows.reshape(VOLUMES, row_count, 4)
        partial_grads = lax.map(lambda item: backward(*item), (rows, cot_rows, w_in, w_hidden, w_head))
        totals = tuple((total + piece for total, piece in zip(totals, partial_grads)))
        return (totals, color)
    start = (jnp.zeros(w_in.shape, jnp.float32), jnp.zeros(w_hidden.shape, jnp.float32), jnp.zeros(w_head.shape, jnp.float32))
    totals, colors = lax.scan(one_group, start, (group_pos, group_gap, group_ids, group_tgt))
    rendered = jnp.transpose(colors, (2, 0, 1, 3)).reshape(3, N_REP * N_VOL * RAYS_DEV)
    return (rendered, totals[0], totals[1], totals[2])
```

```python
import functools

import jax
import jax.numpy as jnp
from jax import lax
from jax.experimental import pallas as pl
from jax.experimental.pallas import tpu as pltpu
from jax.sharding import PartitionSpec as P

FREQS = 10
COORDS = 3
CHUNK = 4
FORWARD_CHUNK = 2
PAYLOAD = 40
BF = jnp.bfloat16
F32 = jnp.float32

COS_PI = (
    0.9999999889445765,
    -4.9348011166440395,
    4.058694745521683,
    -1.3351580223048074,
    0.23502902262478848,
    -0.025358285754444,
    0.0015936782135993002,
)
COS_TURN = tuple(factor * 4.0**power for power, factor in enumerate(COS_PI))
ROUNDER = 12582912.0

NT = (((1,), (1,)), ((), ()))
TN = (((0,), (0,)), ((), ()))


def mm(left, right):
    return jnp.dot(left, right, preferred_element_type=F32)


def mm_nt(left, right):
    return lax.dot_general(left, right, NT, preferred_element_type=F32)


def split3(values):
    high = values.astype(BF).astype(F32)
    rest = values - high
    middle = rest.astype(BF).astype(F32)
    low = rest - middle
    return jnp.concatenate([high, middle, low], axis=0).astype(BF)


def join3(stacked, count):
    return stacked[:count] + stacked[count : 2 * count] + stacked[2 * count :]


def one_hot_rows(count, row):
    shape = (count, row.shape[1])
    same = lax.broadcasted_iota(jnp.int32, shape, 0) == row
    return jnp.where(same, 1.0, 0.0).astype(BF)


def sigmoid(value):
    return 0.5 + 0.5 * jnp.tanh(0.5 * value)


def softplus(value):
    return jnp.maximum(value, 0.0) + jnp.log1p(jnp.exp(-jnp.abs(value)))


def dispatch_kernel(
    volume_count,
    capacity,
    pos_hbm,
    gap_hbm,
    ids_hbm,
    tgt_hbm,
    out_hbm,
    place_hbm,
    pos_ref,
    gap_ref,
    ids_ref,
    tgt_ref,
    out_ref,
    place_ref,
    sems,
):
    copies = [
        pltpu.make_async_copy(source, target, sems.at[index])
        for index, (source, target) in enumerate(
            [(ids_hbm, ids_ref), (pos_hbm, pos_ref), (gap_hbm, gap_ref), (tgt_hbm, tgt_ref)]
        )
    ]
    for copy in copies:
        copy.start()
    rays = pos_ref.shape[2]
    segs = 2 * rays
    owners, _, width = out_ref.shape
    upper = jnp.where(
        lax.broadcasted_iota(jnp.int32, (segs, segs), 0)
        < lax.broadcasted_iota(jnp.int32, (segs, segs), 1),
        1.0,
        0.0,
    ).astype(BF)
    copies[0].wait()
    ids = jnp.concatenate([ids_ref[0:1, :], ids_ref[1:2, :]], axis=1)
    same = lax.broadcasted_iota(jnp.int32, (volume_count, segs), 0) == ids
    table = jnp.where(same, 1.0, 0.0)
    earlier = mm(table.astype(BF), upper)
    rank = jnp.sum(earlier * table, axis=0, keepdims=True)
    place = ids * capacity + rank.astype(jnp.int32)
    place_ref[...] = place
    place_f = place.astype(F32)
    partner = jnp.concatenate([place_f[:, rays:], place_f[:, :rays]], axis=1)
    second = jnp.where(lax.broadcasted_iota(jnp.int32, (1, segs), 1) >= rays, 1.0, 0.0)
    for copy in copies[1:]:
        copy.wait()
    tgt = tgt_ref[...]
    extra = jnp.concatenate(
        [jnp.concatenate([tgt, tgt], axis=1), partner, second, jnp.zeros((3, segs), F32)], axis=0
    )
    values = jnp.concatenate(
        [
            jnp.concatenate([pos_ref[0], pos_ref[1]], axis=1),
            jnp.concatenate([gap_ref[0], gap_ref[1]], axis=1),
            extra,
        ],
        axis=0,
    )
    writes = [pltpu.make_async_copy(place_ref, place_hbm, sems.at[4])]
    writes[0].start()
    pieces = split3(values)
    half = owners // 2
    for part in range(2):
        hot = one_hot_rows(half * width, place - part * half * width)
        slots = join3(mm_nt(pieces, hot), PAYLOAD)
        for n in range(half):
            out_ref[part * half + n] = slots[:, n * width : (n + 1) * width]
        block = pl.ds(part * half, half)
        writes.append(
            pltpu.make_async_copy(out_ref.at[block], out_hbm.at[block], sems.at[5 + part])
        )
        writes[-1].start()
    for write in writes:
        write.wait()


def selection(samples, start):
    shape = (128, samples * 64)
    source = lax.broadcasted_iota(jnp.int32, shape, 0) + start
    column = lax.broadcasted_iota(jnp.int32, shape, 1)
    sample, entry = column // 64, column % 64
    angle = jnp.where(entry < 30, entry, entry - 30)
    axis = jnp.where(entry < 60, angle // FREQS, entry - 60)
    power = jnp.where(entry < 60, angle % FREQS, 1)
    factor = 0.5 * lax.shift_left(jnp.ones(shape, jnp.int32), power).astype(F32)
    wanted = (source < 72) & (source % 24 == axis * samples + sample) & (entry < 63)
    constant = jnp.where(entry < 30, -0.25, jnp.where(entry == 63, 1.0, 0.0))
    value = jnp.where(wanted, factor, jnp.where(source == 72, constant, 0.0))
    return value.astype(BF)


def wave(turns):
    turns = turns - ((turns + ROUNDER) - ROUNDER)
    square = turns * turns
    value = square * COS_TURN[-1] + COS_TURN[-2]
    for factor in COS_TURN[-3::-1]:
        value = value * square + factor
    return value


def silu(half):
    half = half.astype(BF)
    up = jnp.asarray(1.0, BF) + jnp.tanh(half)
    return half * up, up


def segment_parts(half_raw, gaps):
    samples = gaps.shape[1]
    gates = [
        0.5 + 0.5 * jnp.tanh(half_raw[:, c * samples : (c + 1) * samples]) for c in range(4)
    ]
    tau = softplus(2.0 * half_raw[:, 3 * samples :]) * gaps
    before = [jnp.zeros_like(tau[:, :1])]
    for sample in range(1, samples + 1):
        before.append(before[-1] + tau[:, sample - 1 : sample])
    ahead = jnp.exp(-jnp.concatenate(before[:-1], axis=1))
    thinned = jnp.exp(-tau)
    share = ahead * (1.0 - thinned)
    return gates, ahead, thinned, share, jnp.exp(-before[-1])


def forward_kernel(
    capacity,
    in_ref,
    picks_ref,
    pair_ref,
    w2_ref,
    w3_ref,
    slots_ref,
    enc_t_ref,
    seg_ref,
    send_ref,
    terms_ref,
    *rest,
):
    stored, raw_ref = rest[:-1], rest[-1]
    owners = in_ref.shape[0]
    held, hidden, _ = w2_ref.shape
    features = pair_ref.shape[1] // 2
    samples = 8
    width = owners * capacity
    for vol in range(held):
        for src in range(owners):
            slots_ref[vol, :, src * capacity : (src + 1) * capacity] = in_ref[
                src, :, vol * capacity : (vol + 1) * capacity
            ]
    plain = lax.broadcasted_iota(jnp.int32, (1, samples * features), 1) % features >= 60

    def encode(vol):
        pieces = split3(slots_ref[vol, 0:24, :]).astype(F32)
        points = jnp.concatenate(
            [pieces, jnp.ones((8, width), F32), jnp.zeros((48, width), F32)], axis=0
        )
        turns = mm(points.T.astype(BF), picks_ref[...])
        return jnp.where(plain, turns, wave(turns)).astype(BF)

    def first(enc, i, pair):
        pairs = [enc[:, j * features : (j + 2) * features] for j in range(i, i + FORWARD_CHUNK, 2)]
        both = mm(jnp.concatenate(pairs, axis=0), pair)
        return jnp.concatenate(
            [
                both[n * width : (n + 1) * width, j * hidden : (j + 1) * hidden]
                for n in range(FORWARD_CHUNK // 2)
                for j in range(2)
            ],
            axis=0,
        )

    order = [(vol, i) for vol in range(held) for i in range(0, samples, FORWARD_CHUNK)]
    enc, half_one, act_one, half_two = {0: encode(0)}, {}, {}, {}
    for step in range(len(order) + 3):
        stores = []
        if step < len(order):
            vol, i = order[step]
            half_one[step] = first(enc[vol], i, pair_ref[vol])
            if i == 0 and vol + 1 < held:
                enc[vol + 1] = encode(vol + 1)
            turned = enc[vol][:, i * features : (i + FORWARD_CHUNK) * features].T
            for j in range(FORWARD_CHUNK):
                lanes = pl.ds((i + j) * width, width)
                stores.append(
                    (enc_t_ref.at[vol, :, lanes], turned[j * features : (j + 1) * features])
                )
        at = step - 2
        if 0 <= at < len(order):
            half_two[at] = mm(act_one.pop(at), w2_ref[order[at][0]])
        at = step - 1
        if 0 <= at < len(order):
            vol, i = order[at]
            act_one[at], up = silu(half_one.pop(at))
            rows = pl.ds(i * width, FORWARD_CHUNK * width)
            stores.append((stored[4 * vol].at[rows, :], act_one[at]))
            stores.append((stored[4 * vol + 2].at[rows, :], up))
        at = step - 3
        if 0 <= at < len(order):
            vol, i = order[at]
            act_two, up = silu(half_two.pop(at))
            rows = pl.ds(i * width, FORWARD_CHUNK * width)
            stores.append((stored[4 * vol + 1].at[rows, :], act_two))
            stores.append((stored[4 * vol + 3].at[rows, :], up))
            values = mm(act_two, w3_ref[vol])
            for j in range(FORWARD_CHUNK):
                part = values[j * width : (j + 1) * width]
                raw = part if i + j == 0 else raw + pltpu.roll(part, i + j, 1)
            if i + FORWARD_CHUNK == samples:
                stores.append((raw_ref.at[vol], raw.T[: 4 * samples]))
        for ref, value in stores:
            ref[...] = value

    gaps = slots_ref[:, 24:32, :]
    gates, ahead, thinned, share, passing = segment_parts(raw_ref[...], gaps)
    for c in range(3):
        seg_ref[:, c : c + 1, :] = jnp.sum(share * gates[c], axis=1, keepdims=True)
    seg_ref[:, 3:4, :] = passing
    seg_ref[:, 4:, :] = jnp.zeros((held, 4, width), F32)
    terms = gates[:3] + [share * (gate * (1.0 - gate)) for gate in gates[:3]]
    terms += [share, ahead * thinned, gaps * gates[3]]
    for index, term in enumerate(terms):
        terms_ref[:, index * samples : (index + 1) * samples, :] = term
    for src in range(owners):
        lanes = slice(src * capacity, (src + 1) * capacity)
        send_ref[pl.ds(src, 4, stride=owners), :] = jnp.concatenate(
            [seg_ref[vol, 0:4, lanes] for vol in range(held)], axis=1
        )


def table_lane(place, slot_width, me, low, high):
    owner = place // slot_width
    apart = owner ^ me
    position = (apart % low) * high + apart // low
    return position * slot_width + (place - owner * slot_width)


def prepare_kernel(vols, order, slot_width, *refs):
    where_ref, slots_ref = refs[:2]
    stored = refs[2 : 2 + 4 * len(vols)]
    outs = refs[2 + 4 * len(vols) :]
    samples = 8
    width = slots_ref.shape[2]
    me = where_ref[1]
    hidden = stored[0].shape[1]
    eye = one_hot_rows(hidden, lax.broadcasted_iota(jnp.int32, (1, hidden), 1))
    for n, vol in enumerate(vols):
        slope_one_ref, slope_two_ref, hot_ref, act_t_ref = outs[4 * n : 4 * n + 4]
        act_one = stored[4 * n][0:width, :]
        turned = mm_nt(eye, act_one)
        for i in range(samples):
            rows = slice(i * width, (i + 1) * width)
            act_two, up_one, up_two = [ref[rows, :] for ref in stored[4 * n + 1 : 4 * n + 4]]
            if i + 1 < samples:
                act_next = stored[4 * n][(i + 1) * width : (i + 2) * width, :]
                turned_next = mm_nt(eye, act_next)
            slopes = []
            for act, up in ((act_one, up_one), (act_two, up_two)):
                slopes.append(up + act * (jnp.asarray(2.0, BF) - up))
            slope_one_ref[rows, :] = slopes[0]
            slope_two_ref[rows, :] = slopes[1]
            act_t_ref[:, rows] = turned.astype(BF)
            act_one, turned = act_next, turned_next
        partner = slots_ref[vol, 35:36, :].astype(jnp.int32)
        hot_ref[...] = one_hot_rows(hot_ref.shape[0], table_lane(partner, slot_width, me, *order))


def gathered(all_ref, owners):
    count = all_ref.shape[0] // owners
    return split3(
        jnp.concatenate([all_ref[n * count : (n + 1) * count] for n in range(owners)], axis=1)
    )


def look_up(pieces, hot, owners, is_source):
    found = join3(mm(pieces, hot), 4 * owners)
    return [
        jnp.sum(
            jnp.where(is_source, found[c * owners : (c + 1) * owners], 0.0), axis=0, keepdims=True
        )
        for c in range(4)
    ]


def color_kernel(owners, order, slot_width, where_ref, place_ref, all_ref, color_ref):
    rays = color_ref.shape[1]
    hot = one_hot_rows(
        owners * slot_width, table_lane(place_ref[...], slot_width, where_ref[1], *order)
    )
    own_row = lax.broadcasted_iota(jnp.int32, (owners, 2 * rays), 0) == where_ref[1]
    values = look_up(gathered(all_ref, owners), hot, owners, own_row)
    for c in range(3):
        color_ref[c : c + 1, :] = values[c][:, :rays] + values[3][:, :rays] * values[c][:, rays:]


def cotangents(
    capacity, owners, replicas, all_ref, slots_ref, seg_ref, terms_ref, hot_refs, cots_ref
):
    samples = 8
    width = owners * capacity
    pieces = gathered(all_ref, owners)
    source = lax.broadcasted_iota(jnp.int32, (owners, width), 1) // capacity
    is_source = lax.broadcasted_iota(jnp.int32, (owners, width), 0) == source

    for vol in range(slots_ref.shape[0]):
        extra = slots_ref[vol, 32:40, :]
        other = look_up(pieces, hot_refs[vol][...], owners, is_source)
        seg = seg_ref[vol]
        own = [seg[c : c + 1] for c in range(4)]
        is_second = extra[4:5] > 0.5
        cot_color = []
        cot_pass = jnp.zeros((1, width), F32)
        for c in range(3):
            color = jnp.where(
                is_second, other[c] + other[3] * own[c], own[c] + own[3] * other[c]
            )
            cot = (color - extra[c : c + 1]) / replicas
            cot_color.append(jnp.where(is_second, cot * other[3], cot))
            cot_pass = cot_pass + cot * other[c]
        cot_pass = jnp.where(is_second, 0.0, cot_pass)

        terms = [
            terms_ref[vol, index * samples : (index + 1) * samples, :] for index in range(9)
        ]
        pull = jnp.zeros((samples, width), F32)
        raw_cots = []
        for c in range(3):
            pull = pull + cot_color[c] * terms[c]
            raw_cots.append(cot_color[c] * terms[3 + c])
        weighted = pull * terms[6]
        behind = [jnp.zeros((1, width), F32)]
        for sample in range(samples - 1, 0, -1):
            behind.insert(0, behind[0] + weighted[sample : sample + 1])
        cot_tau = pull * terms[7] - jnp.concatenate(behind, axis=0) - cot_pass * own[3]
        raw_cots.append(cot_tau * terms[8])
        for i in range(samples):
            cots_ref[vol, :, i * width : (i + 1) * width] = jnp.concatenate(
                [raw_cots[c][i : i + 1] for c in range(4)] + [jnp.zeros((4, width), F32)], axis=0
            )


def backward_kernel(capacity, owners, replicas, vols, given, form, *refs):
    where_ref, w2_ref, w3_ref, enc_t_ref = refs[:4]
    prepared = [refs[4 + 4 * n : 8 + 4 * n] for n in range(len(vols))]
    rest = refs[4 + 4 * len(vols) :]
    if form == "pairs":
        held = w2_ref.shape[0]
        sources, rest = rest[: 4 + held], rest[4 + held :]
    else:
        cots_ref, rest = rest[0], rest[1:]
    given_refs, rest = rest[: 3 * given], rest[3 * given :]
    out_refs, grad_hidden_s = rest[:-1], rest[-1]
    if form == "pairs":
        cots_ref, out_refs = out_refs[-1], out_refs[:-1]
        cotangents(capacity, owners, replicas, *sources[:4], sources[4:], cots_ref)
    hidden = w2_ref.shape[1]
    features = enc_t_ref.shape[1]
    samples = 8
    width = owners * capacity
    block = hidden // replicas
    group = where_ref[0]

    def last(n, vol, i):
        cots = cots_ref[vol, :, i * width : (i + CHUNK) * width].T.astype(BF)
        return mm(cots, w3_ref[vol])

    order = [(n, vol, i) for n, vol in enumerate(vols) for i in range(0, samples, CHUNK)]
    pulled = last(*order[0])
    hiddens, ins, heads = [], [], []
    for at, (n, vol, i) in enumerate(order):
        rows = slice(i * width, (i + CHUNK) * width)
        act_two_ref, slope_one_ref, slope_two_ref, act_t_ref = prepared[n]
        slope_one, slope_two = slope_one_ref[rows, :], slope_two_ref[rows, :]
        act_two = act_two_ref[rows, :]
        act_t, enc_t, w2 = act_t_ref[:, rows], enc_t_ref[vol, :, rows], w2_ref[vol]
        cots = cots_ref[vol, :, rows].astype(BF)
        ahead = last(*order[at + 1]) if at + 1 < len(order) else None
        cot_two = pulled.astype(BF) * slope_two
        cot_one = mm_nt(cot_two, w2)
        sums = [mm(act_t, cot_two), mm(cots, act_two)]
        sums.append(mm(enc_t, cot_one.astype(BF) * slope_one))
        for total, part in zip((hiddens, heads, ins), sums):
            if i == 0:
                total.append(part)
            else:
                total[n] = total[n] + part
        pulled = ahead
    for n in range(len(vols)):
        grad_hidden_s[n] = hiddens[n]

    if form == "raw":
        for n in range(len(vols)):
            out_refs[3 * n][...] = grad_hidden_s[n]
            out_refs[3 * n + 1][...] = ins[n]
            out_refs[3 * n + 2][...] = heads[n]
        return
    hiddens = [given_refs[3 * n] for n in range(given)]
    hiddens += [grad_hidden_s.at[n] for n in range(len(vols))]
    ins = [given_refs[3 * n + 1][...] for n in range(given)] + ins
    heads = [given_refs[3 * n + 2][...] for n in range(given)] + heads
    count = len(hiddens)
    base = count * block
    half = features // 2
    if form == "pairs":
        targets = [
            (out_refs[way].at[k], group ^ way, 2 * k)
            for way in range(2)
            for k in range(replicas // 2)
        ]
    else:
        targets = [(out_refs[k], group, k) for k in range(replicas)]
    for out_ref, start, k in targets:
        to = pl.ds(pl.multiple_of(lax.rem(start + k, replicas) * block, block), block)
        for n in range(count):
            out_ref[n * block : (n + 1) * block, :] = hiddens[n][to, :].astype(BF)
        turn = jnp.where(start == 0, 0, hidden - start * block)
        cols = slice(k * block, (k + 1) * block)
        parts = [
            pltpu.roll(grad, turn, 1)[h * half : (h + 1) * half, cols]
            for grad in ins
            for h in range(2)
        ]
        out_ref[base : base + half, : 2 * count * block] = jnp.concatenate(parts, axis=1).astype(BF)
        head = jnp.concatenate([pltpu.roll(grad, turn, 1)[:, cols] for grad in heads], axis=1)
        out_ref[base + half :, : count * block] = jnp.concatenate(
            [head, jnp.zeros_like(head)], axis=0
        ).astype(BF)


def sum_kernel(addends, *refs):
    grad_in_ref, grad_hidden_ref, grad_head_ref = refs[-3:]
    held, features, block = grad_in_ref.shape
    half = features // 2
    count = held // len(addends)
    base = count * block
    start = 0
    for part, number in enumerate(addends):
        pieces = refs[start : start + number]
        start += number
        total = pieces[0][...].astype(F32)
        for piece in pieces[1:]:
            total = total + piece[...].astype(F32)
        for v in range(count):
            vol = part * count + v
            grad_hidden_ref[vol] = total[v * block : (v + 1) * block]
            for h in range(2):
                cols = slice((2 * v + h) * block, (2 * v + h + 1) * block)
                grad_in_ref[vol, h * half : (h + 1) * half, :] = total[base : base + half, cols]
            grad_head_ref[vol] = total[base + half : base + half + 4, v * block : (v + 1) * block]


VMEM = pl.BlockSpec(memory_space=pltpu.VMEM)
SMEM = pl.BlockSpec(memory_space=pltpu.SMEM)
HBM = pl.BlockSpec(memory_space=pltpu.HBM)


def call(kernel, specs, inputs, out_shape, scratch=(), limit=16, flops=0, out_space=VMEM):
    return pl.pallas_call(
        kernel,
        out_shape=out_shape,
        in_specs=list(specs),
        out_specs=jax.tree.map(lambda _: out_space, out_shape),
        scratch_shapes=list(scratch),
        compiler_params=pltpu.CompilerParams(vmem_limit_bytes=limit << 20),
        cost_estimate=pl.CostEstimate(flops=flops, bytes_accessed=flops >> 10, transcendentals=0),
    )(*inputs)


def steps(count, size):
    return [(at, (at + count) % size) for at in range(size)]


def local(positions, spacing, volume_ids, target, w_in, w_hidden, w_head):
    rays, seg_count = volume_ids.shape
    samples = spacing.shape[2]
    owners = lax.axis_size("vol")
    replicas = lax.axis_size("rep")
    held, features, hidden = w_in.shape
    volume_count = owners * held
    capacity = 2 * rays * seg_count // volume_count
    slot_width = held * capacity
    width = owners * capacity
    rows = width * samples
    shape = jax.ShapeDtypeStruct
    where = jnp.stack([lax.axis_index("rep"), lax.axis_index("vol")]).astype(jnp.int32)

    outgoing, place = call(
        functools.partial(dispatch_kernel, volume_count, capacity),
        [HBM] * 4,
        (
            jnp.transpose(positions, (1, 2, 0)),
            jnp.transpose(spacing, (1, 2, 0)),
            volume_ids.T,
            target,
        ),
        (
            shape((owners, PAYLOAD, slot_width), F32),
            shape((1, rays * seg_count), jnp.int32),
        ),
        limit=60,
        scratch=(
            pltpu.VMEM((seg_count, COORDS * samples, rays), F32),
            pltpu.VMEM((seg_count, samples, rays), F32),
            pltpu.VMEM((seg_count, rays), jnp.int32),
            pltpu.VMEM((3, rays), F32),
            pltpu.VMEM((owners, PAYLOAD, slot_width), F32),
            pltpu.VMEM((1, rays * seg_count), jnp.int32),
            pltpu.SemaphoreType.DMA((7,)),
        ),
        out_space=HBM,
    )
    outgoing, late_in, late_hidden, late_head, zero = lax.optimization_barrier(
        (outgoing, w_in, w_hidden, w_head, jnp.zeros((), jnp.int32))
    )
    arrived = lax.all_to_all(outgoing, "vol", split_axis=0, concat_axis=0, tiled=True)
    half = jnp.asarray(0.5, BF)
    half_in = late_in * half
    pair = jnp.pad(half_in, ((0, 0), (0, features), (0, hidden))) + jnp.pad(
        half_in, ((0, 0), (features, 0), (hidden, 0))
    )
    half_hidden, half_head = late_hidden * half, late_head * half
    w_head_t = lax.pad(
        jnp.swapaxes(half_head, 1, 2),
        jnp.zeros((), BF),
        ((0, 0, 0), (0, 0, 0), (0, 127 - 3 * samples, samples - 1)),
    )
    w_head_8 = jnp.pad(half_head, ((0, 0), (0, 4), (0, 0)))
    slots, enc_t, seg, gathering, terms, *stored = call(
        functools.partial(forward_kernel, capacity),
        [VMEM] * 5,
        (arrived, selection(samples, zero), pair, half_hidden, w_head_t),
        (
            shape((held, PAYLOAD, width), F32),
            shape((held, features, rows), BF),
            shape((held, 8, width), F32),
            shape((4 * owners, slot_width), F32),
            shape((held, 9 * samples, width), F32),
        )
        + (shape((rows, hidden), BF),) * (4 * held),
        scratch=(pltpu.VMEM((held, 4 * samples, width), F32),),
        flops=10**10,
    )

    low = 1 << ((owners.bit_length() - 1) // 2)
    high = owners // low
    order = (low, high)
    prepared, hots = {}, {}
    for stage, (stride, count) in enumerate(((low, high), (1, low))):
        received = [
            lax.ppermute(gathering, "vol", [(at, at ^ (n * stride)) for at in range(owners)])
            for n in range(count - 1, 0, -1)
        ][::-1]
        vols = list(range(stage * held // 2, (stage + 1) * held // 2))
        late_slots = lax.optimization_barrier((slots, gathering))[0] if stage else slots
        outs = call(
            functools.partial(prepare_kernel, vols, order, slot_width),
            [SMEM] + [VMEM] * (1 + 4 * len(vols)),
            (where, late_slots) + tuple(stored[4 * vols[0] : 4 * vols[-1] + 4]),
            (
                shape((rows, hidden), BF),
                shape((rows, hidden), BF),
                shape((volume_count * capacity, width), BF),
                shape((hidden, rows), BF),
            )
            * len(vols),
            flops=len(vols) * 3 * 10**9,
        )
        outs = tuple(outs)
        *received, first_out = lax.optimization_barrier(tuple(received) + (outs[2],))
        outs = outs[:2] + (first_out,) + outs[3:]
        for n, vol in enumerate(vols):
            slope_one, slope_two, hots[vol], act_t = outs[4 * n : 4 * n + 4]
            prepared[vol] = (stored[4 * vol + 1], slope_one, slope_two, act_t)
        gathering = jnp.concatenate([gathering] + received, axis=0)

    block = hidden // replicas
    count = held // 2
    send_rows = count * block + features // 2 + 16

    def backward(vols, given, form, outs):
        given = tuple(given)
        return call(
            functools.partial(
                backward_kernel, capacity, owners, replicas, vols, len(given) // 3, form
            ),
            [SMEM] + [VMEM] * (3 + 4 * len(vols) + len(sources) + len(given)),
            (where, half_hidden, w_head_8, enc_t)
            + sum((prepared[vol] for vol in vols), ())
            + sources
            + given,
            outs,
            scratch=(pltpu.VMEM((len(vols), hidden, hidden), F32),),
            flops=len(vols) * 5 * 10**9,
        )

    sources = (gathering, slots, seg, terms) + tuple(hots[vol] for vol in range(held))
    keep, give, cots = backward(
        list(range(count)),
        (),
        "pairs",
        (shape((replicas // 2, send_rows, hidden), BF),) * 2 + (shape((held, 8, rows), F32),),
    )
    sources = (cots,)
    received = lax.ppermute(give, "rep", [(at, at ^ 1) for at in range(replicas)])
    middle = list(range(count, held - 1))
    raw_grads = ()
    if middle:
        raw_grads = backward(
            middle,
            (),
            "raw",
            (
                shape((hidden, hidden), F32),
                shape((features, hidden), F32),
                shape((8, hidden), F32),
            )
            * len(middle),
        )
        received, *raw_grads = lax.optimization_barrier((received,) + tuple(raw_grads))
    total = keep.astype(F32) + received.astype(F32)
    pieces = [total[0]]
    for k in range(1, replicas // 2):
        pieces.append(lax.ppermute(total[k].astype(BF), "rep", steps(2 * k, replicas)))
    cots, raw_grads, total = lax.optimization_barrier((cots, raw_grads, total))
    sources = (cots,)
    outs = backward(
        [held - 1], raw_grads, "direct", (shape((send_rows, hidden), BF),) * replicas
    )
    pieces.append(outs[0])
    for k in range(1, replicas):
        pieces.append(lax.ppermute(outs[k], "rep", steps(k, replicas)))
    late, _ = lax.optimization_barrier((gathering, outs[0]))
    color = call(
        functools.partial(color_kernel, owners, order, slot_width),
        [SMEM, VMEM, VMEM],
        (where, place, late),
        shape((3, rays), F32),
    )
    grad_in, grad_hidden, grad_head = call(
        functools.partial(sum_kernel, (replicas // 2, replicas)),
        [VMEM] * len(pieces),
        pieces,
        (
            shape((held, features, block), F32),
            shape((held, block, hidden), F32),
            shape((held, 4, block), F32),
        ),
    )
    return color, grad_in, grad_hidden, grad_head


def solution(mesh):
    return jax.shard_map(
        local,
        mesh=mesh,
        in_specs=(
            P(("rep", "vol"), None, None),
            P(("rep", "vol"), None, None),
            P(("rep", "vol"), None),
            P(None, ("rep", "vol")),
            P("vol", None, None),
            P("vol", None, None),
            P("vol", None, None),
        ),
        out_specs=(
            P(None, ("rep", "vol")),
            P("vol", None, "rep"),
            P("vol", "rep", None),
            P("vol", None, "rep"),
        ),
        check_vma=False,
    )
```

```python
import functools

import jax
import jax.numpy as jnp
from jax import lax
from jax.experimental import pallas as pl
from jax.experimental.pallas import tpu as pltpu
from jax.sharding import PartitionSpec as P

FREQS = 10
COORDS = 3
CHUNK = 4
FORWARD_CHUNK = 2
PAYLOAD = 40
BF = jnp.bfloat16
F32 = jnp.float32

COS_PI = (
    0.9999999889445765,
    -4.9348011166440395,
    4.058694745521683,
    -1.3351580223048074,
    0.23502902262478848,
    -0.025358285754444,
    0.0015936782135993002,
)
COS_TURN = tuple(factor * 4.0**power for power, factor in enumerate(COS_PI))
ROUNDER = 12582912.0

NT = (((1,), (1,)), ((), ()))
TN = (((0,), (0,)), ((), ()))


def mm(left, right):
    return jnp.dot(left, right, preferred_element_type=F32)


def mm_nt(left, right):
    return lax.dot_general(left, right, NT, preferred_element_type=F32)


def split3(values):
    high = values.astype(BF).astype(F32)
    rest = values - high
    middle = rest.astype(BF).astype(F32)
    low = rest - middle
    return jnp.concatenate([high, middle, low], axis=0).astype(BF)


def join3(stacked, count):
    return stacked[:count] + stacked[count : 2 * count] + stacked[2 * count :]


def one_hot_rows(count, row):
    shape = (count, row.shape[1])
    same = lax.broadcasted_iota(jnp.int32, shape, 0) == row
    return jnp.where(same, 1.0, 0.0).astype(BF)


def sigmoid(value):
    return 0.5 + 0.5 * jnp.tanh(0.5 * value)


def softplus(value):
    return jnp.maximum(value, 0.0) + jnp.log1p(jnp.exp(-jnp.abs(value)))


def dispatch_kernel(
    volume_count,
    capacity,
    pos_hbm,
    gap_hbm,
    ids_hbm,
    tgt_hbm,
    out_hbm,
    place_hbm,
    pos_ref,
    gap_ref,
    ids_ref,
    tgt_ref,
    out_ref,
    place_ref,
    sems,
):
    copies = [
        pltpu.make_async_copy(source, target, sems.at[index])
        for index, (source, target) in enumerate(
            [(ids_hbm, ids_ref), (pos_hbm, pos_ref), (gap_hbm, gap_ref), (tgt_hbm, tgt_ref)]
        )
    ]
    for copy in copies:
        copy.start()
    rays = pos_ref.shape[2]
    segs = 2 * rays
    owners, _, width = out_ref.shape
    upper = jnp.where(
        lax.broadcasted_iota(jnp.int32, (segs, segs), 0)
        < lax.broadcasted_iota(jnp.int32, (segs, segs), 1),
        1.0,
        0.0,
    ).astype(BF)
    copies[0].wait()
    ids = jnp.concatenate([ids_ref[0:1, :], ids_ref[1:2, :]], axis=1)
    same = lax.broadcasted_iota(jnp.int32, (volume_count, segs), 0) == ids
    table = jnp.where(same, 1.0, 0.0)
    earlier = mm(table.astype(BF), upper)
    rank = jnp.sum(earlier * table, axis=0, keepdims=True)
    place = ids * capacity + rank.astype(jnp.int32)
    place_ref[...] = place
    place_f = place.astype(F32)
    partner = jnp.concatenate([place_f[:, rays:], place_f[:, :rays]], axis=1)
    second = jnp.where(lax.broadcasted_iota(jnp.int32, (1, segs), 1) >= rays, 1.0, 0.0)
    for copy in copies[1:]:
        copy.wait()
    tgt = tgt_ref[...]
    extra = jnp.concatenate(
        [jnp.concatenate([tgt, tgt], axis=1), partner, second, jnp.zeros((3, segs), F32)], axis=0
    )
    values = jnp.concatenate(
        [
            jnp.concatenate([pos_ref[0], pos_ref[1]], axis=1),
            jnp.concatenate([gap_ref[0], gap_ref[1]], axis=1),
            extra,
        ],
        axis=0,
    )
    writes = [pltpu.make_async_copy(place_ref, place_hbm, sems.at[4])]
    writes[0].start()
    pieces = split3(values)
    half = owners // 2
    for part in range(2):
        hot = one_hot_rows(half * width, place - part * half * width)
        slots = join3(mm_nt(pieces, hot), PAYLOAD)
        for n in range(half):
            out_ref[part * half + n] = slots[:, n * width : (n + 1) * width]
        block = pl.ds(part * half, half)
        writes.append(
            pltpu.make_async_copy(out_ref.at[block], out_hbm.at[block], sems.at[5 + part])
        )
        writes[-1].start()
    for write in writes:
        write.wait()


def selection(samples, start):
    shape = (128, samples * 64)
    source = lax.broadcasted_iota(jnp.int32, shape, 0) + start
    column = lax.broadcasted_iota(jnp.int32, shape, 1)
    sample, entry = column // 64, column % 64
    angle = jnp.where(entry < 30, entry, entry - 30)
    axis = jnp.where(entry < 60, angle // FREQS, entry - 60)
    power = jnp.where(entry < 60, angle % FREQS, 1)
    factor = 0.5 * lax.shift_left(jnp.ones(shape, jnp.int32), power).astype(F32)
    wanted = (source < 72) & (source % 24 == axis * samples + sample) & (entry < 63)
    constant = jnp.where(entry < 30, -0.25, jnp.where(entry == 63, 1.0, 0.0))
    value = jnp.where(wanted, factor, jnp.where(source == 72, constant, 0.0))
    return value.astype(BF)


def wave(turns):
    turns = turns - ((turns + ROUNDER) - ROUNDER)
    square = turns * turns
    value = square * COS_TURN[-1] + COS_TURN[-2]
    for factor in COS_TURN[-3::-1]:
        value = value * square + factor
    return value


def silu(half):
    half = half.astype(BF)
    up = jnp.asarray(1.0, BF) + jnp.tanh(half)
    return half * up, up


def segment_parts(half_raw, gaps):
    samples = gaps.shape[1]
    gates = [
        0.5 + 0.5 * jnp.tanh(half_raw[:, c * samples : (c + 1) * samples]) for c in range(4)
    ]
    tau = softplus(2.0 * half_raw[:, 3 * samples :]) * gaps
    before = [jnp.zeros_like(tau[:, :1])]
    for sample in range(1, samples + 1):
        before.append(before[-1] + tau[:, sample - 1 : sample])
    ahead = jnp.exp(-jnp.concatenate(before[:-1], axis=1))
    thinned = jnp.exp(-tau)
    share = ahead * (1.0 - thinned)
    return gates, ahead, thinned, share, jnp.exp(-before[-1])


def forward_kernel(
    capacity,
    in_ref,
    picks_ref,
    pair_ref,
    w2_ref,
    w3_ref,
    slots_ref,
    enc_ref,
    seg_ref,
    send_ref,
    terms_ref,
    *rest,
):
    stored, raw_ref = rest[:-1], rest[-1]
    owners = in_ref.shape[0]
    held, hidden, _ = w2_ref.shape
    features = pair_ref.shape[1] // 2
    samples = 8
    width = owners * capacity
    lane = lax.broadcasted_iota(jnp.int32, (1, 128), 1)
    plain = lax.broadcasted_iota(jnp.int32, (1, samples * features), 1) % features >= 60

    def encode(vol):
        for src in range(owners):
            slots_ref[vol, :, src * capacity : (src + 1) * capacity] = in_ref[
                src, :, vol * capacity : (vol + 1) * capacity
            ]
        pieces = split3(slots_ref[vol, 0:24, :]).astype(F32)
        points = jnp.concatenate(
            [pieces, jnp.ones((8, width), F32), jnp.zeros((48, width), F32)], axis=0
        )
        turns = mm(points.T.astype(BF), picks_ref[...])
        return jnp.where(plain, turns, wave(turns)).astype(BF)

    def first(enc, i, pair):
        pairs = [enc[:, j * features : (j + 2) * features] for j in range(i, i + FORWARD_CHUNK, 2)]
        both = mm(jnp.concatenate(pairs, axis=0), pair)
        return jnp.concatenate(
            [
                both[n * width : (n + 1) * width, j * hidden : (j + 1) * hidden]
                for n in range(FORWARD_CHUNK // 2)
                for j in range(2)
            ],
            axis=0,
        )

    order = [(vol, i) for vol in range(held) for i in range(0, samples, FORWARD_CHUNK)]
    enc, half_one, act_one, half_two = {0: encode(0)}, {}, {}, {}
    for step in range(len(order) + 3):
        stores = []
        if step < len(order):
            vol, i = order[step]
            half_one[step] = first(enc[vol], i, pair_ref[vol])
            if i == 0 and vol + 1 < held:
                enc[vol + 1] = encode(vol + 1)
            if i == 0:
                stores.append((enc_ref.at[vol], enc[vol]))
        at = step - 2
        if 0 <= at < len(order):
            half_two[at] = mm(act_one.pop(at), w2_ref[order[at][0]])
        at = step - 1
        if 0 <= at < len(order):
            vol, i = order[at]
            act_one[at], up = silu(half_one.pop(at))
            rows = pl.ds(i * width, FORWARD_CHUNK * width)
            stores.append((stored[4 * vol].at[rows, :], act_one[at]))
            stores.append((stored[4 * vol + 2].at[rows, :], up))
        at = step - 3
        if 0 <= at < len(order):
            vol, i = order[at]
            act_two, up = silu(half_two.pop(at))
            rows = pl.ds(i * width, FORWARD_CHUNK * width)
            stores.append((stored[4 * vol + 1].at[rows, :], act_two))
            stores.append((stored[4 * vol + 3].at[rows, :], up))
            side = jnp.concatenate(
                [act_two[j * width : (j + 1) * width] for j in range(FORWARD_CHUNK)], axis=1
            )
            spread = w3_ref[vol]
            layers = [
                jnp.where(lane % samples == i + j, spread, jnp.zeros((), BF))
                for j in range(FORWARD_CHUNK)
            ]
            part = mm(side, jnp.concatenate(layers, axis=0))
            raw = part if i == 0 else raw + part
            if i + FORWARD_CHUNK == samples:
                stores.append((raw_ref.at[vol], raw.T[: 4 * samples]))
        for ref, value in stores:
            ref[...] = value

    gaps = slots_ref[:, 24:32, :]
    gates, ahead, thinned, share, passing = segment_parts(raw_ref[...], gaps)
    for c in range(3):
        seg_ref[:, c : c + 1, :] = jnp.sum(share * gates[c], axis=1, keepdims=True)
    seg_ref[:, 3:4, :] = passing
    seg_ref[:, 4:, :] = jnp.zeros((held, 4, width), F32)
    terms = gates[:3] + [share * (gate * (1.0 - gate)) for gate in gates[:3]]
    terms += [share, ahead * thinned, gaps * gates[3]]
    for index, term in enumerate(terms):
        terms_ref[:, index * samples : (index + 1) * samples, :] = term
    for src in range(owners):
        lanes = slice(src * capacity, (src + 1) * capacity)
        send_ref[pl.ds(src, 4, stride=owners), :] = jnp.concatenate(
            [seg_ref[vol, 0:4, lanes] for vol in range(held)], axis=1
        )


def table_lane(place, slot_width, me, low, high):
    owner = place // slot_width
    apart = owner ^ me
    position = (apart % low) * high + apart // low
    return position * slot_width + (place - owner * slot_width)


def prepare_kernel(vols, order, slot_width, *refs):
    where_ref, slots_ref, enc_ref = refs[:3]
    stored = refs[3 : 3 + 4 * len(vols)]
    outs = refs[3 + 4 * len(vols) :]
    samples = 8
    width = slots_ref.shape[2]
    me = where_ref[1]
    hidden = stored[0].shape[1]
    eye = one_hot_rows(hidden, lax.broadcasted_iota(jnp.int32, (1, hidden), 1))
    for n, vol in enumerate(vols):
        slope_one_ref, slope_two_ref, hot_ref, act_t_ref, enc_t_ref = outs[5 * n : 5 * n + 5]
        features = enc_t_ref.shape[0]
        act_one = stored[4 * n][0:width, :]
        turned = mm_nt(eye, act_one)
        for i in range(samples):
            rows = slice(i * width, (i + 1) * width)
            act_two, up_one, up_two = [ref[rows, :] for ref in stored[4 * n + 1 : 4 * n + 4]]
            if i + 1 < samples:
                act_next = stored[4 * n][(i + 1) * width : (i + 2) * width, :]
                turned_next = mm_nt(eye, act_next)
            slopes = []
            for act, up in ((act_one, up_one), (act_two, up_two)):
                slopes.append(up + act * (jnp.asarray(2.0, BF) - up))
            slope_one_ref[rows, :] = slopes[0]
            slope_two_ref[rows, :] = slopes[1]
            act_t_ref[:, rows] = turned.astype(BF)
            if i % 2 == 0:
                enc = enc_ref[vol, :, i * features : (i + 2) * features].T
                for j in range(2):
                    lanes = slice((i + j) * width, (i + j + 1) * width)
                    enc_t_ref[:, lanes] = enc[j * features : (j + 1) * features]
            act_one, turned = act_next, turned_next
        partner = slots_ref[vol, 35:36, :].astype(jnp.int32)
        hot_ref[...] = one_hot_rows(hot_ref.shape[0], table_lane(partner, slot_width, me, *order))


def gathered(all_ref, owners):
    count = all_ref.shape[0] // owners
    return split3(
        jnp.concatenate([all_ref[n * count : (n + 1) * count] for n in range(owners)], axis=1)
    )


def look_up(pieces, hot, owners, is_source):
    found = join3(mm(pieces, hot), 4 * owners)
    return [
        jnp.sum(
            jnp.where(is_source, found[c * owners : (c + 1) * owners], 0.0), axis=0, keepdims=True
        )
        for c in range(4)
    ]


def color_kernel(owners, order, slot_width, where_ref, place_ref, all_ref, color_ref):
    rays = color_ref.shape[1]
    hot = one_hot_rows(
        owners * slot_width, table_lane(place_ref[...], slot_width, where_ref[1], *order)
    )
    own_row = lax.broadcasted_iota(jnp.int32, (owners, 2 * rays), 0) == where_ref[1]
    values = look_up(gathered(all_ref, owners), hot, owners, own_row)
    for c in range(3):
        color_ref[c : c + 1, :] = values[c][:, :rays] + values[3][:, :rays] * values[c][:, rays:]


def cotangents(
    capacity, owners, replicas, all_ref, slots_ref, seg_ref, terms_ref, hot_refs, cots_ref
):
    samples = 8
    width = owners * capacity
    pieces = gathered(all_ref, owners)
    source = lax.broadcasted_iota(jnp.int32, (owners, width), 1) // capacity
    is_source = lax.broadcasted_iota(jnp.int32, (owners, width), 0) == source

    def volume(vol):
        extra = slots_ref[vol, 32:40, :]
        other = look_up(pieces, hot_refs[vol][...], owners, is_source)
        seg = seg_ref[vol]
        own = [seg[c : c + 1] for c in range(4)]
        is_second = extra[4:5] > 0.5
        cot_color = []
        cot_pass = jnp.zeros((1, width), F32)
        for c in range(3):
            color = jnp.where(
                is_second, other[c] + other[3] * own[c], own[c] + own[3] * other[c]
            )
            cot = (color - extra[c : c + 1]) / replicas
            cot_color.append(jnp.where(is_second, cot * other[3], cot))
            cot_pass = cot_pass + cot * other[c]
        cot_pass = jnp.where(is_second, 0.0, cot_pass)

        terms = [
            terms_ref[vol, index * samples : (index + 1) * samples, :] for index in range(9)
        ]
        pull = jnp.zeros((samples, width), F32)
        raw_cots = []
        for c in range(3):
            pull = pull + cot_color[c] * terms[c]
            raw_cots.append(cot_color[c] * terms[3 + c])
        weighted = pull * terms[6]
        behind = [jnp.zeros((1, width), F32)]
        for sample in range(samples - 1, 0, -1):
            behind.insert(0, behind[0] + weighted[sample : sample + 1])
        cot_tau = pull * terms[7] - jnp.concatenate(behind, axis=0) - cot_pass * own[3]
        raw_cots.append(cot_tau * terms[8])
        for i in range(samples):
            cots_ref[vol, :, i * width : (i + 1) * width] = jnp.concatenate(
                [raw_cots[c][i : i + 1] for c in range(4)] + [jnp.zeros((4, width), F32)], axis=0
            )

    return volume


def backward_kernel(capacity, owners, replicas, vols, given, form, *refs):
    where_ref, w2_ref, w3_ref = refs[:3]
    prepared = [refs[3 + 5 * n : 8 + 5 * n] for n in range(len(vols))]
    rest = refs[3 + 5 * len(vols) :]
    if form == "pairs":
        held = w2_ref.shape[0]
        sources, rest = rest[: 4 + held], rest[4 + held :]
    else:
        cots_ref, rest = rest[0], rest[1:]
    given_refs, rest = rest[: 3 * given], rest[3 * given :]
    out_refs, grad_hidden_s = rest[:-1], rest[-1]
    if form == "pairs":
        cots_ref, out_refs = out_refs[-1], out_refs[:-1]
        work_out = cotangents(capacity, owners, replicas, *sources[:4], sources[4:], cots_ref)
        work_out(vols[0])
        waiting = [vol for vol in range(held) if vol != vols[0]]
    else:
        waiting = []
    hidden = w2_ref.shape[1]
    features = prepared[0][4].shape[0]
    samples = 8
    width = owners * capacity
    block = hidden // replicas
    group = where_ref[0]

    def last(n, vol, i):
        cots = cots_ref[vol, :, i * width : (i + CHUNK) * width].T.astype(BF)
        return mm(cots, w3_ref[vol])

    order = [(n, vol, i) for n, vol in enumerate(vols) for i in range(0, samples, CHUNK)]
    pulled = last(*order[0])
    hiddens, ins, heads = [], [], []
    for at, (n, vol, i) in enumerate(order):
        rows = slice(i * width, (i + CHUNK) * width)
        act_two_ref, slope_one_ref, slope_two_ref, act_t_ref, enc_t_ref = prepared[n]
        slope_one, slope_two = slope_one_ref[rows, :], slope_two_ref[rows, :]
        act_two = act_two_ref[rows, :]
        act_t, enc_t, w2 = act_t_ref[:, rows], enc_t_ref[:, rows], w2_ref[vol]
        cots = cots_ref[vol, :, rows].astype(BF)
        ahead = last(*order[at + 1]) if at + 1 < len(order) else None
        cot_two = pulled.astype(BF) * slope_two
        cot_one = mm_nt(cot_two, w2)
        sums = [mm(act_t, cot_two), mm(cots, act_two)]
        sums.append(mm(enc_t, cot_one.astype(BF) * slope_one))
        for total, part in zip((hiddens, heads, ins), sums):
            if i == 0:
                total.append(part)
            else:
                total[n] = total[n] + part
        pulled = ahead
        if waiting:
            work_out(waiting.pop(0))
    while waiting:
        work_out(waiting.pop(0))
    for n in range(len(vols)):
        grad_hidden_s[n] = hiddens[n]

    if form == "raw":
        for n in range(len(vols)):
            out_refs[3 * n][...] = grad_hidden_s[n]
            out_refs[3 * n + 1][...] = ins[n]
            out_refs[3 * n + 2][...] = heads[n]
        return
    hiddens = [given_refs[3 * n] for n in range(given)]
    hiddens += [grad_hidden_s.at[n] for n in range(len(vols))]
    ins = [given_refs[3 * n + 1][...] for n in range(given)] + ins
    heads = [given_refs[3 * n + 2][...] for n in range(given)] + heads
    count = len(hiddens)
    base = count * block
    half = features // 2
    if form == "pairs":
        targets = [
            (out_refs[way].at[k], group ^ way, 2 * k)
            for way in range(2)
            for k in range(replicas // 2)
        ]
    else:
        targets = [(out_refs[k], group, k) for k in range(replicas)]
    for out_ref, start, k in targets:
        to = pl.ds(pl.multiple_of(lax.rem(start + k, replicas) * block, block), block)
        for n in range(count):
            out_ref[n * block : (n + 1) * block, :] = hiddens[n][to, :].astype(BF)
        turn = jnp.where(start == 0, 0, hidden - start * block)
        cols = slice(k * block, (k + 1) * block)
        parts = [
            pltpu.roll(grad, turn, 1)[h * half : (h + 1) * half, cols]
            for grad in ins
            for h in range(2)
        ]
        out_ref[base : base + half, : 2 * count * block] = jnp.concatenate(parts, axis=1).astype(BF)
        head = jnp.concatenate([pltpu.roll(grad, turn, 1)[:, cols] for grad in heads], axis=1)
        out_ref[base + half :, : count * block] = jnp.concatenate(
            [head, jnp.zeros_like(head)], axis=0
        ).astype(BF)


def sum_kernel(addends, *refs):
    grad_in_ref, grad_hidden_ref, grad_head_ref = refs[-3:]
    held, features, block = grad_in_ref.shape
    half = features // 2
    count = held // len(addends)
    base = count * block
    start = 0
    for part, number in enumerate(addends):
        pieces = refs[start : start + number]
        start += number
        total = pieces[0][...].astype(F32)
        for piece in pieces[1:]:
            total = total + piece[...].astype(F32)
        for v in range(count):
            vol = part * count + v
            grad_hidden_ref[vol] = total[v * block : (v + 1) * block]
            for h in range(2):
                cols = slice((2 * v + h) * block, (2 * v + h + 1) * block)
                grad_in_ref[vol, h * half : (h + 1) * half, :] = total[base : base + half, cols]
            grad_head_ref[vol] = total[base + half : base + half + 4, v * block : (v + 1) * block]


VMEM = pl.BlockSpec(memory_space=pltpu.VMEM)
SMEM = pl.BlockSpec(memory_space=pltpu.SMEM)
HBM = pl.BlockSpec(memory_space=pltpu.HBM)


def call(kernel, specs, inputs, out_shape, scratch=(), limit=16, flops=0, out_space=VMEM):
    return pl.pallas_call(
        kernel,
        out_shape=out_shape,
        in_specs=list(specs),
        out_specs=jax.tree.map(lambda _: out_space, out_shape),
        scratch_shapes=list(scratch),
        compiler_params=pltpu.CompilerParams(vmem_limit_bytes=limit << 20),
        cost_estimate=pl.CostEstimate(flops=flops, bytes_accessed=flops >> 10, transcendentals=0),
    )(*inputs)


def steps(count, size):
    return [(at, (at + count) % size) for at in range(size)]


def local(positions, spacing, volume_ids, target, w_in, w_hidden, w_head):
    rays, seg_count = volume_ids.shape
    samples = spacing.shape[2]
    owners = lax.axis_size("vol")
    replicas = lax.axis_size("rep")
    held, features, hidden = w_in.shape
    volume_count = owners * held
    capacity = 2 * rays * seg_count // volume_count
    slot_width = held * capacity
    width = owners * capacity
    rows = width * samples
    shape = jax.ShapeDtypeStruct
    where = jnp.stack([lax.axis_index("rep"), lax.axis_index("vol")]).astype(jnp.int32)

    outgoing, place = call(
        functools.partial(dispatch_kernel, volume_count, capacity),
        [HBM] * 4,
        (
            jnp.transpose(positions, (1, 2, 0)),
            jnp.transpose(spacing, (1, 2, 0)),
            volume_ids.T,
            target,
        ),
        (
            shape((owners, PAYLOAD, slot_width), F32),
            shape((1, rays * seg_count), jnp.int32),
        ),
        limit=60,
        scratch=(
            pltpu.VMEM((seg_count, COORDS * samples, rays), F32),
            pltpu.VMEM((seg_count, samples, rays), F32),
            pltpu.VMEM((seg_count, rays), jnp.int32),
            pltpu.VMEM((3, rays), F32),
            pltpu.VMEM((owners, PAYLOAD, slot_width), F32),
            pltpu.VMEM((1, rays * seg_count), jnp.int32),
            pltpu.SemaphoreType.DMA((7,)),
        ),
        out_space=HBM,
    )
    outgoing, late_in, late_hidden, late_head, zero = lax.optimization_barrier(
        (outgoing, w_in, w_hidden, w_head, jnp.zeros((), jnp.int32))
    )
    arrived = lax.all_to_all(outgoing, "vol", split_axis=0, concat_axis=0, tiled=True)
    half = jnp.asarray(0.5, BF)
    half_in = late_in * half
    pair = jnp.pad(half_in, ((0, 0), (0, features), (0, hidden))) + jnp.pad(
        half_in, ((0, 0), (features, 0), (hidden, 0))
    )
    half_hidden, half_head = late_hidden * half, late_head * half
    w_head_t = jnp.pad(
        jnp.repeat(jnp.swapaxes(half_head, 1, 2), samples, axis=2),
        ((0, 0), (0, 0), (0, 128 - 4 * samples)),
    )
    w_head_8 = jnp.pad(half_head, ((0, 0), (0, 4), (0, 0)))
    slots, enc, seg, gathering, terms, *stored = call(
        functools.partial(forward_kernel, capacity),
        [VMEM] * 5,
        (arrived, selection(samples, zero), pair, half_hidden, w_head_t),
        (
            shape((held, PAYLOAD, width), F32),
            shape((held, width, samples * features), BF),
            shape((held, 8, width), F32),
            shape((4 * owners, slot_width), F32),
            shape((held, 9 * samples, width), F32),
        )
        + (shape((rows, hidden), BF),) * (4 * held),
        scratch=(pltpu.VMEM((held, 4 * samples, width), F32),),
        flops=10**10,
    )

    low = 1 << ((owners.bit_length() - 1) // 2)
    high = owners // low
    order = (low, high)
    prepared, hots = {}, {}
    for stage, (stride, count) in enumerate(((low, high), (1, low))):
        received = [
            lax.ppermute(gathering, "vol", [(at, at ^ (n * stride)) for at in range(owners)])
            for n in range(count - 1, 0, -1)
        ][::-1]
        vols = list(range(stage * held // 2, (stage + 1) * held // 2))
        late_slots = lax.optimization_barrier((slots, gathering))[0] if stage else slots
        outs = call(
            functools.partial(prepare_kernel, vols, order, slot_width),
            [SMEM] + [VMEM] * (2 + 4 * len(vols)),
            (where, late_slots, enc) + tuple(stored[4 * vols[0] : 4 * vols[-1] + 4]),
            (
                shape((rows, hidden), BF),
                shape((rows, hidden), BF),
                shape((volume_count * capacity, width), BF),
                shape((hidden, rows), BF),
                shape((features, rows), BF),
            )
            * len(vols),
            flops=len(vols) * 3 * 10**9,
        )
        outs = tuple(outs)
        *received, first_out = lax.optimization_barrier(tuple(received) + (outs[2],))
        outs = outs[:2] + (first_out,) + outs[3:]
        for n, vol in enumerate(vols):
            slope_one, slope_two, hots[vol], act_t, enc_t = outs[5 * n : 5 * n + 5]
            prepared[vol] = (stored[4 * vol + 1], slope_one, slope_two, act_t, enc_t)
        gathering = jnp.concatenate([gathering] + received, axis=0)

    block = hidden // replicas
    count = held // 2
    send_rows = count * block + features // 2 + 16

    def backward(vols, given, form, outs):
        given = tuple(given)
        return call(
            functools.partial(
                backward_kernel, capacity, owners, replicas, vols, len(given) // 3, form
            ),
            [SMEM] + [VMEM] * (2 + 5 * len(vols) + len(sources) + len(given)),
            (where, half_hidden, w_head_8)
            + sum((prepared[vol] for vol in vols), ())
            + sources
            + given,
            outs,
            scratch=(pltpu.VMEM((len(vols), hidden, hidden), F32),),
            flops=len(vols) * 5 * 10**9,
        )

    sources = (gathering, slots, seg, terms) + tuple(hots[vol] for vol in range(held))
    keep, give, cots = backward(
        list(range(count)),
        (),
        "pairs",
        (shape((replicas // 2, send_rows, hidden), BF),) * 2 + (shape((held, 8, rows), F32),),
    )
    sources = (cots,)
    received = lax.ppermute(give, "rep", [(at, at ^ 1) for at in range(replicas)])
    middle = list(range(count, held - 1))
    raw_grads = ()
    if middle:
        raw_grads = backward(
            middle,
            (),
            "raw",
            (
                shape((hidden, hidden), F32),
                shape((features, hidden), F32),
                shape((8, hidden), F32),
            )
            * len(middle),
        )
        received, *raw_grads = lax.optimization_barrier((received,) + tuple(raw_grads))
    total = keep.astype(F32) + received.astype(F32)
    pieces = [total[0]]
    for k in range(1, replicas // 2):
        pieces.append(lax.ppermute(total[k].astype(BF), "rep", steps(2 * k, replicas)))
    cots, raw_grads, total = lax.optimization_barrier((cots, raw_grads, total))
    sources = (cots,)
    outs = backward(
        [held - 1], raw_grads, "direct", (shape((send_rows, hidden), BF),) * replicas
    )
    pieces.append(outs[0])
    for k in range(1, replicas):
        pieces.append(lax.ppermute(outs[k], "rep", steps(k, replicas)))
    late, _ = lax.optimization_barrier((gathering, outs[0]))
    color = call(
        functools.partial(color_kernel, owners, order, slot_width),
        [SMEM, VMEM, VMEM],
        (where, place, late),
        shape((3, rays), F32),
    )
    grad_in, grad_hidden, grad_head = call(
        functools.partial(sum_kernel, (replicas // 2, replicas)),
        [VMEM] * len(pieces),
        pieces,
        (
            shape((held, features, block), F32),
            shape((held, block, hidden), F32),
            shape((held, 4, block), F32),
        ),
    )
    return color, grad_in, grad_hidden, grad_head


def solution(mesh):
    return jax.shard_map(
        local,
        mesh=mesh,
        in_specs=(
            P(("rep", "vol"), None, None),
            P(("rep", "vol"), None, None),
            P(("rep", "vol"), None),
            P(None, ("rep", "vol")),
            P("vol", None, None),
            P("vol", None, None),
            P("vol", None, None),
        ),
        out_specs=(
            P(None, ("rep", "vol")),
            P("vol", None, "rep"),
            P("vol", "rep", None),
            P("vol", None, "rep"),
        ),
        check_vma=False,
    )
```
